32 devices in a mesh: cx: 4 (over z), cy: 8 (over y, x, core).
Axes of the slice: x: 2, y: 2, z: 4, core: 2. Of those that a mesh axis runs over, the one named last changes fastest.
Arguments:
- points_block: bfloat16 [256, 64, 256], P(('cx', 'cy')), may hold values from -6 to 6
- leaf_basis: bfloat16 [256, 64, 256], P(('cx', 'cy')), may hold values from -0.375 to 0.375
- near_blocks: bfloat16 [256, 4, 256, 256], P(('cx', 'cy')), may hold values from -0.1875 to 0.1875
- near_ids: int32 [256, 4], P(('cx', 'cy')), may hold values from 0 to 255, as said below
- local_transfer: bfloat16 [224, 128, 64], P(('cx', 'cy')), may hold values from -0.5 to 0.5
- far_coupling: bfloat16 [256, 8, 64, 64], P(('cx', 'cy')), may hold values from -0.25 to 0.25
- far_ids: int32 [256, 8], P(('cx', 'cy')), may hold values from 0 to 255, as said below
- upper_transfer: bfloat16 [31, 128, 64], replicated, may hold values from -0.5 to 0.5
- upper_coupling: bfloat16 [31, 64, 64], replicated, may hold values from -0.75 to 0.75
Outputs:
- product: bfloat16 [256, 64, 256], P(('cx', 'cy'))
The draws below stay inside these ranges and needn't reach their ends.
Inputs may be any that keep to these rules, and one draw needn't show every extreme that they name: `near_ids`: slot 0 of each leaf is the leaf itself; every id names a leaf of the same device or of the two devices before or after it, devices numbered in the order cx then cy. `far_ids`: every id names a leaf of the same device or of the two devices before or after it, devices numbered in the order cx then cy.
All inputs are finite; a program needn't handle non-finite values.
Results may differ from the reference program's by a relative error of at most 0.004.
Values may be sent and summed in bfloat16 or wider, within the bound.
A program may use at most 128 MiB of HBM per device.

```python
import jax
import jax.numpy as jnp
from jax import lax

LEAF = 256
RANK = 64
COLS = 64
KNEAR = 4
KFAR = 8
LDEV = 8
NLEAF = 256
N_CX = 4
N_CY = 8


def window_ids(key, count):
    leaves = jnp.arange(NLEAF, dtype=jnp.int32)
    owner = leaves // LDEV
    lowest = jnp.maximum(owner - 2, 0) * LDEV
    highest = jnp.minimum(owner + 3, NLEAF // LDEV) * LDEV
    raw_ids = jax.random.randint(key, (NLEAF, count), 0, 1 << 20, dtype=jnp.int32)
    picked = lowest[:, None] + raw_ids % (highest - lowest)[:, None]
    picked = picked.at[0, count - 1].set(0)
    picked = picked.at[NLEAF - 1, count - 1].set(NLEAF - 1)
    return (picked, leaves)


def draw_near_ids(key, part):
    picked, leaves = window_ids(jax.random.fold_in(key, 11), KNEAR)
    return picked.at[:, 0].set(leaves)


def draw_far_ids(key, part):
    picked, leaves = window_ids(jax.random.fold_in(key, 23), KFAR)
    return picked


def level_of(own_key, shape, split, low, top_value):
    loudness = 1.0
    for axis_at, blocks in split:
        draws = jax.random.uniform(jax.random.fold_in(jax.random.fold_in(own_key, 6), axis_at), (blocks,), jnp.float32, low / len(split), top_value / len(split))
        loudness = loudness * jnp.repeat(jnp.exp(draws), shape[axis_at] // blocks).reshape((-1,) + (1,) * (len(shape) - 1 - axis_at))
    return loudness


def noise(key, shape, deviation, most, split=(), kind=jnp.bfloat16):
    drawn = jax.random.normal(key, shape, jnp.float32) * deviation
    if len(split) > 0:
        drawn = level_of(key, shape, split, -0.22, 0.18) * drawn
    return jnp.clip(drawn, min=-most, max=most).astype(kind)


def setup_inputs(seed: int = 0) -> dict:
    splits = jax.random.split(jax.random.key(seed), 10)
    points_block = noise(splits[0], (NLEAF, COLS, LEAF), 1.0, 6.0, ((0, 32),))
    leaf_basis = noise(splits[1], (NLEAF, RANK, LEAF), LEAF ** -0.5, 0.375, ((0, 32),))
    near_blocks = noise(splits[2], (NLEAF, KNEAR, LEAF, LEAF), (LEAF * KNEAR) ** -0.5, 0.1875, ((0, 32),))
    near_ids = draw_near_ids(jax.random.fold_in(splits[9], 71), 0)
    local_transfer = noise(splits[4], ((LDEV - 1) * N_CX * N_CY, 2 * RANK, RANK), (2 * RANK) ** -0.5, 0.5, ((0, 32),))
    far_coupling = noise(splits[5], (NLEAF, KFAR, RANK, RANK), (RANK * KFAR) ** -0.5, 0.25, ((0, 32),))
    far_ids = draw_far_ids(jax.random.fold_in(splits[9], 71), 0)
    upper_transfer = noise(splits[7], (N_CX * N_CY - 1, 2 * RANK, RANK), (2 * RANK) ** -0.5, 0.5)
    upper_coupling = noise(splits[8], (N_CX * N_CY - 1, RANK, RANK), RANK ** -0.5, 0.75)
    return {"points_block": points_block, "leaf_basis": leaf_basis, "near_blocks": near_blocks, "near_ids": near_ids, "local_transfer": local_transfer, "far_coupling": far_coupling, "far_ids": far_ids, "upper_transfer": upper_transfer, "upper_coupling": upper_coupling}


def up_level(transfer, children):
    count = transfer.shape[0]
    stacked = children.reshape(count, 2 * children.shape[1], children.shape[2])
    return jnp.einsum('nkr,nkc->nrc', transfer, stacked, precision=lax.Precision.HIGHEST)


def down_level(transfer, parents):
    count = transfer.shape[0]
    out_rows = jnp.einsum('nkr,nrc->nkc', transfer, parents, precision=lax.Precision.HIGHEST)
    return out_rows.reshape(2 * count, transfer.shape[2], parents.shape[2])


def upper_tree(roots, upper_transfer, upper_coupling):
    count = roots.shape[0]
    offset = 0
    skeleton = roots
    saved = []
    while count > 1:
        half = count // 2
        transfer = upper_transfer[offset:offset + half].astype(jnp.float32)
        coupling = upper_coupling[offset:offset + half].astype(jnp.float32)
        pairs = skeleton.reshape(half, 2, skeleton.shape[1], skeleton.shape[2])
        to_left = jnp.einsum('nab,nbc->nac', coupling, pairs[:, 1], precision=lax.Precision.HIGHEST)
        to_right = jnp.einsum('nba,nbc->nac', coupling, pairs[:, 0], precision=lax.Precision.HIGHEST)
        terms = jnp.stack([to_left, to_right], 1).reshape(count, skeleton.shape[1], skeleton.shape[2])
        saved.append((transfer, terms))
        skeleton = up_level(transfer, skeleton)
        offset = offset + half
        count = half
    coeffs = jnp.zeros_like(skeleton)
    for transfer, terms in reversed(saved):
        coeffs = down_level(transfer, coeffs) + terms
    return coeffs


def reference(points_block, leaf_basis, near_blocks, near_ids, local_transfer, far_coupling, far_ids, upper_transfer, upper_coupling):
    devices = N_CX * N_CY
    skel_leaf = jnp.einsum('lrp,lcp->lrc', leaf_basis.astype(jnp.float32), points_block.astype(jnp.float32), precision=lax.Precision.HIGHEST)
    skel_half = lax.optimization_barrier(skel_leaf.astype(jnp.bfloat16)).astype(jnp.float32)
    local_all = local_transfer.astype(jnp.float32).reshape(devices, LDEV - 1, 2 * RANK, RANK)
    skeleton = skel_leaf
    offset = 0
    width = LDEV // 2
    local_levels = []
    while width >= 1:
        transfer = local_all[:, offset:offset + width].reshape(devices * width, 2 * RANK, RANK)
        local_levels.append(transfer)
        skeleton = up_level(transfer, skeleton)
        offset = offset + width
        width = width // 2
    coeffs = upper_tree(skeleton, upper_transfer, upper_coupling)
    for transfer in reversed(local_levels):
        coeffs = down_level(transfer, coeffs)

    def per_group(inputs):
        basis, blocks, near_rows, coupling, far_rows, leaf_coeffs = inputs
        far_skel = skel_half[far_rows]
        leafcoef = leaf_coeffs + jnp.einsum('lkab,lkbc->lac', coupling.astype(jnp.float32), far_skel, precision=lax.Precision.HIGHEST)
        coef_half = lax.optimization_barrier(leafcoef.astype(jnp.bfloat16)).astype(jnp.float32)
        far_part = jnp.einsum('lrp,lrc->lcp', basis.astype(jnp.float32), coef_half, precision=lax.Precision.HIGHEST)
        near_cols = points_block[near_rows].astype(jnp.float32)
        near_part = jnp.einsum('lkcq,lkpq->lcp', near_cols, blocks.astype(jnp.float32), precision=lax.Precision.HIGHEST)
        return (far_part + near_part).astype(jnp.bfloat16)

    grouped = (leaf_basis.reshape(devices, LDEV, RANK, LEAF),
               near_blocks.reshape(devices, LDEV, KNEAR, LEAF, LEAF),
               near_ids.reshape(devices, LDEV, KNEAR),
               far_coupling.reshape(devices, LDEV, KFAR, RANK, RANK),
               far_ids.reshape(devices, LDEV, KFAR),
               coeffs.reshape(devices, LDEV, RANK, COLS))
    result = lax.map(per_group, grouped)
    return result.reshape(NLEAF, COLS, LEAF)
```

```python
import functools

import jax
import jax.numpy as jnp
from jax import lax
from jax.experimental import pallas as pl
from jax.experimental.pallas import tpu as pltpu
from jax.sharding import PartitionSpec as P

F32 = jnp.float32
BF16 = jnp.bfloat16
CHUNKS = 2
REACH = 2


def levels_of(count):
    return count.bit_length() - 1


def kernel(
    n_cx,
    n_cy,
    near_ids,
    far_ids,
    points,
    basis,
    near,
    local_transfer,
    far,
    upper_transfer,
    upper_coupling,
    out,
    win_cols,
    win_skel,
    basis_v,
    near_v,
    local_v,
    far_v,
    upper_v,
    coup_v,
    acc,
    leaf_pairs,
    group,
    roots,
    load_sem,
    cols_send,
    cols_recv,
    mate_send,
    mate_recv,
    relay_send,
    relay_recv,
    skel_send,
    skel_recv,
    group_send,
    group_recv,
    root_send,
    root_recv,
):
    leaves, cols, leaf = points.shape
    rank = basis.shape[1]
    knear, kfar = near.shape[1], far.shape[1]
    n = n_cx * n_cy
    cx, cy = lax.axis_index("cx"), lax.axis_index("cy")
    me = cx * n_cy + cy
    odd = lax.rem(me, 2)
    mate = me + 1 - 2 * odd
    up_group, up_all = levels_of(n_cy), levels_of(n)

    def at(position):
        return (lax.div(position, n_cy), lax.rem(position, n_cy))

    loads = []

    def load(src, dst):
        copy = pltpu.make_async_copy(src, dst, load_sem.at[len(loads)])
        copy.start()
        loads.append(copy)
        return copy

    own = pl.ds(REACH * leaves, leaves)
    get_points = load(points, win_cols.at[own])
    get_basis = load(basis, basis_v)
    get_local = load(local_transfer, local_v)
    get_upper = []
    offset, kept = 0, 0
    starts = []
    for level in range(1, up_all):
        width = n >> level
        here = max(n_cy >> level, 1) if level <= up_group else width
        first = offset + (cx * here if level <= up_group else 0)
        starts.append(kept)
        get_upper.append(
            load(upper_transfer.at[pl.ds(first, here)], upper_v.at[pl.ds(kept, here)])
        )
        kept += here
        offset += width
    get_coup = []
    offset = 0
    for level in range(1, up_all + 1):
        row = offset + lax.div(me, 1 << level)
        get_coup.append(load(upper_coupling.at[row], coup_v.at[level - 1]))
        offset += n >> level
    get_near = load(near, near_v)
    get_far = load(far, far_v)

    barrier = pltpu.get_barrier_semaphore()
    for j in range(1, n_cy):
        pl.semaphore_signal(
            barrier, inc=1, device_id=(cx, lax.rem(cy + j, n_cy)), device_id_type=pl.DeviceIdType.MESH
        )
    for j in range(1, n_cx):
        pl.semaphore_signal(
            barrier, inc=1, device_id=(lax.rem(cx + j, n_cx), cy), device_id_type=pl.DeviceIdType.MESH
        )

    def exists(by):
        return me >= -by if by < 0 else me + by < n

    def outside(by):
        edge = cy < -by if by < 0 else cy + by >= n_cy
        return jnp.logical_and(exists(by), edge)

    offsets = (2, -2, 1, -1)
    for by in offsets:

        @pl.when(outside(by))
        def _(by=by):
            pl.semaphore_signal(
                barrier, inc=1, device_id=at(me + by), device_id_type=pl.DeviceIdType.MESH
            )

    peers = n_cy - 1 + n_cx - 1
    for by in offsets:
        peers = peers + jnp.where(outside(by), 1, 0)
    pl.semaphore_wait(barrier, peers)

    def remote(src, dst, send, recv, target):
        return pltpu.make_async_remote_copy(
            src_ref=src,
            dst_ref=dst,
            send_sem=send,
            recv_sem=recv,
            device_id=target,
            device_id_type=pl.DeviceIdType.MESH,
        )

    size = leaves // CHUNKS

    def piece(slot, chunk):
        return win_cols.at[pl.ds(slot * leaves + chunk * size, size)]

    def cols_copy(which, chunk):
        by = (2, -2)[which]
        return remote(
            piece(REACH, chunk),
            piece(REACH - by, chunk),
            cols_send.at[which, chunk],
            cols_recv.at[which, chunk],
            at(me + by),
        )

    mate_copy = remote(
        win_cols.at[own],
        win_cols.at[pl.ds((REACH - 1 + 2 * odd) * leaves, leaves)],
        mate_send,
        mate_recv,
        at(mate),
    )

    def relay_copy(chunk):
        return remote(
            piece(4 - 4 * odd, chunk),
            piece(3 - 2 * odd, chunk),
            relay_send.at[chunk],
            relay_recv.at[chunk],
            at(mate),
        )

    get_points.wait()
    for chunk in range(CHUNKS):
        for which, by in enumerate((2, -2)):

            @pl.when(exists(by))
            def _(which=which, chunk=chunk):
                cols_copy(which, chunk).start()

    mate_copy.start()

    lane = lax.broadcasted_iota(jnp.int32, (rank, 2 * cols), 1)
    low = lane < cols

    def fold(x):
        return x + pltpu.roll(x, cols, 1)

    def pack(s):
        hi = s.astype(BF16).astype(F32)
        return jnp.where(low, hi, s - hi).astype(BF16)

    def dot(a, b):
        return lax.dot_general(a, b, (((1,), (0,)), ((), ())), preferred_element_type=F32)

    def dot_t(a, b):
        return lax.dot_general(a, b, (((0,), (0,)), ((), ())), preferred_element_type=F32)

    def up(transfer, left, right):
        return pack(fold(dot_t(transfer, jnp.concatenate([left, right], 0))))

    get_basis.wait()
    skels = []
    half = leaves // 2
    for pair in range(half):
        both = []
        for g in (2 * pair, 2 * pair + 1):
            tile = win_cols[REACH * leaves + g]
            both.append(
                lax.dot_general(
                    basis_v[g],
                    jnp.concatenate([tile, tile], 0),
                    (((1,), (1,)), ((), ())),
                    preferred_element_type=F32,
                )
            )
        win_skel[REACH * half + pair] = jnp.where(low, both[0], both[1]).astype(BF16)
        skels += [pack(s) for s in both]

    def skel_copy(which):
        by = offsets[which]
        return remote(
            win_skel.at[pl.ds(REACH * half, half)],
            win_skel.at[pl.ds((REACH - by) * half, half)],
            skel_send.at[which],
            skel_recv.at[which],
            at(me + by),
        )

    get_local.wait()
    row = 0
    width = half
    current = skels
    while width >= 1:
        current = [
            up(local_v[row + m], current[2 * m], current[2 * m + 1]) for m in range(width)
        ]
        row += width
        width //= 2
    group[cy] = current[0]

    def group_copy(j):
        return remote(
            group.at[cy],
            group.at[cy],
            group_send.at[j],
            group_recv.at[j],
            (cx, lax.rem(cy + j, n_cy)),
        )

    def root_copy(j):
        return remote(
            roots.at[cx],
            roots.at[cx],
            root_send.at[j],
            root_recv.at[j],
            (lax.rem(cx + j, n_cx), cy),
        )

    def group_arrival(j):
        source = lax.rem(cy + n_cy - j, n_cy)
        return remote(
            group.at[source], group.at[source], group_send.at[j], group_recv.at[j], (cx, source)
        )

    def root_arrival(j):
        source = lax.rem(cx + n_cx - j, n_cx)
        return remote(
            roots.at[source], roots.at[source], root_send.at[j], root_recv.at[j], (source, cy)
        )

    for j in range(1, n_cy):
        group_copy(j).start()
    for which, by in enumerate(offsets):

        @pl.when(exists(by))
        def _(which=which):
            skel_copy(which).start()

    for copy in get_upper + get_coup:
        copy.wait()

    def path_term(level, sibling):
        right = lax.rem(lax.div(me, 1 << (level - 1)), 2)
        coupling = coup_v[level - 1].astype(F32)
        turned = jnp.where(right == 1, coupling.T, coupling).astype(BF16)
        return fold(dot(turned, sibling))

    for j in range(1, n_cy):
        group_arrival(j).wait_recv()
    terms = []
    saved = group
    base = 0
    nodes = n_cy
    for level in range(1, up_group + 1):
        nodes //= 2
        for m in range(nodes):
            made = up(
                upper_v[starts[level - 1] + m], saved[base + 2 * m], saved[base + 2 * m + 1]
            )
            if nodes > 1:
                leaf_pairs[(n_cy - 2 * nodes) + m] = made
            else:
                roots[cx] = made
        if nodes > 1:
            saved, base = leaf_pairs, n_cy - 2 * nodes
    for j in range(1, n_cx):
        root_copy(j).start()

    def sibling_at(level):
        mine = lax.div(cy, 1 << (level - 1))
        return mine + 1 - 2 * lax.rem(mine, 2)

    base = 0
    nodes = n_cy
    for level in range(1, up_group + 1):
        if level == 1:
            sibling = group[sibling_at(level)]
        else:
            sibling = leaf_pairs[base + sibling_at(level)]
        terms.append(path_term(level, sibling))
        nodes //= 2
        base = n_cy - 2 * nodes

    get_near.wait()

    def near_dot(tile, block):
        return lax.dot_general(
            tile, block, (((1,), (1,)), ((), ())), preferred_element_type=F32
        )

    def own_near(g, _):
        acc[g] = near_dot(win_cols[REACH * leaves + g], near_v[g, 0])
        return 0

    lax.fori_loop(0, leaves, own_near, 0)

    for j in range(1, n_cx):
        root_arrival(j).wait_recv()

    if n_cx > 1:
        for x in range(n_cx):
            leaf_pairs[n_cy + x] = roots[x]
        base, nodes = n_cy, n_cx
        fresh = n_cy + n_cx
        for level in range(up_group + 1, up_all + 1):
            mine = lax.div(cx, 1 << (level - up_group - 1))
            sibling = leaf_pairs[base + mine + 1 - 2 * lax.rem(mine, 2)]
            terms.append(path_term(level, sibling))
            nodes //= 2
            if nodes > 1:
                for m in range(nodes):
                    leaf_pairs[fresh + m] = up(
                        upper_v[starts[level - 1] + m],
                        leaf_pairs[base + 2 * m],
                        leaf_pairs[base + 2 * m + 1],
                    )
                base = fresh
                fresh += nodes

    coef = terms[-1]
    for level in range(up_all - 1, 0, -1):
        place = lax.div(cy, 1 << level) if level <= up_group else lax.div(me, 1 << level)
        right = lax.rem(lax.div(me, 1 << (level - 1)), 2)
        rows = upper_v[starts[level - 1] + place, pl.ds(pl.multiple_of(right * rank, rank), rank)]
        coef = fold(dot(rows, pack(coef))) + terms[level - 1]
    coefs = [coef]
    width = 1
    row = leaves - 1
    while width < leaves:
        row -= width
        following = []
        for m in range(width):
            made = fold2(dot(local_v[row + m], pack(coefs[m])), cols)
            following += [made[:rank], made[rank:]]
        coefs = following
        width *= 2

    for which, by in enumerate(offsets):

        @pl.when(exists(-by))
        def _(which=which):
            skel_copy(which).wait_recv()

    get_far.wait()
    first = (me - REACH) * leaves

    def slot_of(leaf_id):
        return jnp.clip(leaf_id - first, 0, (2 * REACH + 1) * leaves - 1)

    high_row = (lax.broadcasted_iota(jnp.int32, (1, 2 * cols), 1) >= cols).astype(F32)
    leafcoefs = []
    for g in range(leaves):
        total = None
        for k in range(kfar):
            index = slot_of(far_ids[g, k])
            parity = (index & 1).astype(F32)
            keep = (parity * high_row + (1.0 - parity) * (1.0 - high_row)).astype(BF16)
            term = dot(far_v[g, k], win_skel[index >> 1] * keep)
            total = term if total is None else total + term
        leafcoef = coefs[g] + fold(total)
        coef_half = leafcoef[:, :cols].astype(BF16)
        acc[g] = acc[g] + dot_t(coef_half, basis_v[g])

    relays = jnp.where(odd == 1, me >= 2, me + 2 < n)
    relayed = jnp.where(odd == 1, me + 2 < n, me >= 2)
    for chunk in range(CHUNKS):
        for which, by in enumerate((2, -2)):

            @pl.when(exists(-by))
            def _(which=which, chunk=chunk):
                cols_copy(which, chunk).wait_recv()

        @pl.when(relays)
        def _(chunk=chunk):
            relay_copy(chunk).start()

    mate_copy.wait_recv()
    for chunk in range(CHUNKS):

        @pl.when(relayed)
        def _(chunk=chunk):
            relay_copy(chunk).wait_recv()

    def far_near(g, _):
        total = acc[g]
        for k in range(1, knear):
            total = total + near_dot(win_cols[slot_of(near_ids[g, k])], near_v[g, k])
        out[g] = total.astype(BF16)
        return 0

    lax.fori_loop(0, leaves, far_near, 0)

    for chunk in range(CHUNKS):
        for which, by in enumerate((2, -2)):

            @pl.when(exists(by))
            def _(which=which, chunk=chunk):
                cols_copy(which, chunk).wait_send()

        @pl.when(relays)
        def _(chunk=chunk):
            relay_copy(chunk).wait_send()

    mate_copy.wait_send()
    for which, by in enumerate(offsets):

        @pl.when(exists(by))
        def _(which=which):
            skel_copy(which).wait_send()

    for j in range(1, n_cy):
        group_copy(j).wait_send()
    for j in range(1, n_cx):
        root_copy(j).wait_send()


def fold2(x, cols):
    return x + pltpu.roll(x, cols, 1)


def solution(mesh):
    n_cx, n_cy = mesh.shape["cx"], mesh.shape["cy"]
    n = n_cx * n_cy

    def local(
        points, basis, near, near_ids, local_transfer, far, far_ids, upper_transfer, upper_coupling
    ):
        leaves, cols, leaf = points.shape
        rank = basis.shape[1]
        up_group, up_all = levels_of(n_cy), levels_of(n)
        window = 2 * REACH + 1
        kept = n_cy + n_cx
        any_space = pl.BlockSpec(memory_space=pl.ANY)
        dma = pltpu.SemaphoreType.DMA
        return pl.pallas_call(
            functools.partial(kernel, n_cx, n_cy),
            out_shape=jax.ShapeDtypeStruct(points.shape, points.dtype),
            in_specs=[pl.BlockSpec(memory_space=pltpu.SMEM)] * 2 + [any_space] * 7,
            out_specs=pl.BlockSpec(memory_space=pltpu.VMEM),
            scratch_shapes=[
                pltpu.VMEM((window * leaves, cols, leaf), BF16),
                pltpu.VMEM((window * leaves // 2, rank, 2 * cols), BF16),
                pltpu.VMEM(basis.shape, BF16),
                pltpu.VMEM(near.shape, BF16),
                pltpu.VMEM(local_transfer.shape, BF16),
                pltpu.VMEM(far.shape, BF16),
                pltpu.VMEM((kept,) + upper_transfer.shape[1:], BF16),
                pltpu.VMEM((up_all,) + upper_coupling.shape[1:], BF16),
                pltpu.VMEM((leaves, cols, leaf), F32),
                pltpu.VMEM((n_cy + 2 * n_cx, rank, 2 * cols), BF16),
                pltpu.VMEM((n_cy, rank, 2 * cols), BF16),
                pltpu.VMEM((n_cx, rank, 2 * cols), BF16),
                dma((5 + 2 * up_all,)),
                dma((2, CHUNKS)),
                dma((2, CHUNKS)),
                dma,
                dma,
                dma((CHUNKS,)),
                dma((CHUNKS,)),
                dma((4,)),
                dma((4,)),
                dma((n_cy,)),
                dma((n_cy,)),
                dma((n_cx,)),
                dma((n_cx,)),
            ],
            compiler_params=pltpu.CompilerParams(
                collective_id=0, has_side_effects=True, vmem_limit_bytes=56 * 2**20
            ),
        )(near_ids, far_ids, points, basis, near, local_transfer, far, upper_transfer, upper_coupling)

    split = ("cx", "cy")
    return jax.shard_map(
        local,
        mesh=mesh,
        in_specs=(
            P(split, None, None),
            P(split, None, None),
            P(split, None, None, None),
            P(split, None),
            P(split, None, None),
            P(split, None, None, None),
            P(split, None),
            P(),
            P(),
        ),
        out_specs=P(split, None, None),
        check_vma=False,
    )
```

```python
import functools

import jax
import jax.numpy as jnp
from jax import lax
from jax.experimental import pallas as pl
from jax.experimental.pallas import tpu as pltpu
from jax.sharding import PartitionSpec as P

F32 = jnp.float32
BF16 = jnp.bfloat16
CHUNKS = 4
REACH = 2


def levels_of(count):
    return count.bit_length() - 1


def kernel(
    n_cx,
    n_cy,
    near_ids,
    far_ids,
    points,
    basis,
    near,
    local_transfer,
    far,
    upper_transfer,
    upper_coupling,
    out,
    win_cols,
    win_skel,
    basis_v,
    near_v,
    local_v,
    far_v,
    upper_v,
    coup_v,
    acc,
    local_down,
    path_down,
    far_sum,
    leaf_pairs,
    group,
    roots,
    load_sem,
    x_send,
    x_recv,
    y_send,
    y_recv,
    mate_send,
    mate_recv,
    relay_send,
    relay_recv,
    group_send,
    group_recv,
    root_send,
    root_recv,
):
    leaves, cols, leaf = points.shape
    rank = basis.shape[1]
    knear, kfar = near.shape[1], far.shape[1]
    n = n_cx * n_cy
    cx, cy = lax.axis_index("cx"), lax.axis_index("cy")
    me = cx * n_cy + cy
    odd = lax.rem(me, 2)
    mate = me + 1 - 2 * odd
    up_group, up_all = levels_of(n_cy), levels_of(n)

    def at(position):
        return (lax.div(position, n_cy), lax.rem(position, n_cy))

    loads = []

    def load(src, dst):
        copy = pltpu.make_async_copy(src, dst, load_sem.at[len(loads)])
        copy.start()
        loads.append(copy)
        return copy

    own = pl.ds(REACH * leaves, leaves)
    get_points = load(points, win_cols.at[own])
    get_basis = load(basis, basis_v)
    get_local = load(local_transfer, local_v)
    get_upper = []
    offset, kept = 0, 0
    starts = []
    for level in range(1, up_all):
        width = n >> level
        here = max(n_cy >> level, 1) if level <= up_group else width
        first = offset + (cx * here if level <= up_group else 0)
        starts.append(kept)
        get_upper.append(
            load(upper_transfer.at[pl.ds(first, here)], upper_v.at[pl.ds(kept, here)])
        )
        kept += here
        offset += width
    get_coup = []
    offset = 0
    for level in range(1, up_all + 1):
        row = offset + lax.div(me, 1 << level)
        get_coup.append(load(upper_coupling.at[row], coup_v.at[level - 1]))
        offset += n >> level
    get_near = load(near, near_v)
    get_far = load(far, far_v)

    barrier = pltpu.get_barrier_semaphore()
    for j in range(1, n_cy):
        pl.semaphore_signal(
            barrier, inc=1, device_id=(cx, lax.rem(cy + j, n_cy)), device_id_type=pl.DeviceIdType.MESH
        )
    for j in range(1, n_cx):
        pl.semaphore_signal(
            barrier, inc=1, device_id=(lax.rem(cx + j, n_cx), cy), device_id_type=pl.DeviceIdType.MESH
        )

    def exists(by):
        return me >= -by if by < 0 else me + by < n

    def outside(by):
        edge = cy < -by if by < 0 else cy + by >= n_cy
        return jnp.logical_and(exists(by), edge)

    for by in (4, -4):

        @pl.when(outside(by))
        def _(by=by):
            pl.semaphore_signal(
                barrier, inc=1, device_id=at(me + by), device_id_type=pl.DeviceIdType.MESH
            )

    def remote(src, dst, send, recv, target):
        return pltpu.make_async_remote_copy(
            src_ref=src,
            dst_ref=dst,
            send_sem=send,
            recv_sem=recv,
            device_id=target,
            device_id_type=pl.DeviceIdType.MESH,
        )

    size = leaves // CHUNKS
    half = leaves // 2
    chip_odd = lax.rem(lax.div(me, 2), 2)
    pair_mate = me + 2 - 4 * chip_odd
    pair_slot, onward_slot = 4 - 4 * chip_odd, 4 * chip_odd
    onward = jnp.where(chip_odd == 0, me + 4 < n, me >= 4)
    incoming = jnp.where(chip_odd == 0, me >= 4, me + 4 < n)
    relays = jnp.where(odd == 1, me >= 2, me + 2 < n)
    relayed = jnp.where(odd == 1, me + 2 < n, me >= 2)
    early = jnp.logical_and(relays, chip_odd == odd)
    late = jnp.logical_and(relays, chip_odd != odd)

    def unit(slot, u):
        if u == CHUNKS:
            return win_skel.at[pl.ds(slot * half, half)]
        return win_cols.at[pl.ds(slot * leaves + u * size, size)]

    def x_copy(u):
        return remote(
            unit(REACH, u), unit(onward_slot, u), x_send.at[u], x_recv.at[u], at(pair_mate)
        )

    def y_copy(u):
        return remote(
            unit(pair_slot, u),
            unit(onward_slot, u),
            y_send.at[u],
            y_recv.at[u],
            at(me + 4 - 8 * chip_odd),
        )

    def relay_copy(u):
        return remote(
            unit(4 - 4 * odd, u), unit(3 - 2 * odd, u), relay_send.at[u], relay_recv.at[u], at(mate)
        )

    def mate_copy(whole, index):
        count = whole.shape[0] // (2 * REACH + 1)
        return remote(
            whole.at[pl.ds(REACH * count, count)],
            whole.at[pl.ds((REACH - 1 + 2 * odd) * count, count)],
            mate_send.at[index],
            mate_recv.at[index],
            at(mate),
        )

    def forward(u):
        x_copy(u).wait_recv()

        @pl.when(onward)
        def _():
            y_copy(u).start()

        @pl.when(early)
        def _():
            relay_copy(u).start()

    def finish(u):
        @pl.when(incoming)
        def _():
            y_copy(u).wait_recv()

        @pl.when(late)
        def _():
            relay_copy(u).start()

    def last(u):
        @pl.when(relayed)
        def _():
            relay_copy(u).wait_recv()

    get_points.wait()
    lane = lax.broadcasted_iota(jnp.int32, (rank, 2 * cols), 1)
    low = lane < cols

    def fold(x):
        return x + pltpu.roll(x, cols, 1)

    def pack(s):
        hi = s.astype(BF16).astype(F32)
        return jnp.where(low, hi, s - hi).astype(BF16)

    def dot(a, b):
        return lax.dot_general(a, b, (((1,), (0,)), ((), ())), preferred_element_type=F32)

    def dot_t(a, b):
        return lax.dot_general(a, b, (((0,), (0,)), ((), ())), preferred_element_type=F32)

    def up(transfer, left, right):
        return pack(fold(dot(transfer, jnp.concatenate([left, right], 0))))

    get_basis.wait()
    skels = []
    for pair in range(half):
        both = []
        for g in (2 * pair, 2 * pair + 1):
            tile = win_cols[REACH * leaves + g]
            both.append(
                lax.dot_general(
                    basis_v[g],
                    jnp.concatenate([tile, tile], 0),
                    (((1,), (1,)), ((), ())),
                    preferred_element_type=F32,
                )
            )
        win_skel[REACH * half + pair] = jnp.where(low, both[0], both[1]).astype(BF16)
        skels += [pack(s) for s in both]

    get_local.wait()
    row = 0
    width = half
    current = skels
    while width >= 1:
        current = [
            up(local_v[row + m], current[2 * m], current[2 * m + 1]) for m in range(width)
        ]
        row += width
        width //= 2
    group[cy] = current[0]

    def group_copy(j):
        return remote(
            group.at[cy],
            group.at[cy],
            group_send.at[j],
            group_recv.at[j],
            (cx, lax.rem(cy + j, n_cy)),
        )

    def root_copy(j):
        return remote(
            roots.at[cx],
            roots.at[cx],
            root_send.at[j],
            root_recv.at[j],
            (lax.rem(cx + j, n_cx), cy),
        )

    def group_arrival(j):
        source = lax.rem(cy + n_cy - j, n_cy)
        return remote(
            group.at[source], group.at[source], group_send.at[j], group_recv.at[j], (cx, source)
        )

    def root_arrival(j):
        source = lax.rem(cx + n_cx - j, n_cx)
        return remote(
            roots.at[source], roots.at[source], root_send.at[j], root_recv.at[j], (source, cy)
        )

    peers = n_cy - 1 + n_cx - 1
    for by in (4, -4):
        peers = peers + jnp.where(outside(by), 1, 0)
    pl.semaphore_wait(barrier, peers)
    for j in range(1, n_cy):
        group_copy(j).start()
    x_copy(CHUNKS).start()
    mate_copy(win_skel, 1).start()
    for u in range(CHUNKS):
        x_copy(u).start()
    mate_copy(win_cols, 0).start()

    for copy in get_upper + get_coup:
        copy.wait()

    def path_term(level, sibling):
        right = lax.rem(lax.div(me, 1 << (level - 1)), 2)
        coupling = coup_v[level - 1].astype(F32)
        turned = jnp.where(right == 1, coupling.T, coupling).astype(BF16)
        return fold(dot(turned, sibling))

    for node in range(leaves - 1):
        local_down[node] = local_v[node].astype(F32).T.astype(BF16)
    for level in range(1, up_all):
        place = lax.div(cy, 1 << level) if level <= up_group else lax.div(me, 1 << level)
        path_down[level - 1] = upper_v[starts[level - 1] + place].astype(F32).T.astype(BF16)

    for j in range(1, n_cy):
        group_arrival(j).wait_recv()
    forward(CHUNKS)
    terms = []
    saved = group
    base = 0
    nodes = n_cy
    for level in range(1, up_group + 1):
        nodes //= 2
        for m in range(nodes):
            made = up(
                upper_v[starts[level - 1] + m], saved[base + 2 * m], saved[base + 2 * m + 1]
            )
            if nodes > 1:
                leaf_pairs[(n_cy - 2 * nodes) + m] = made
            else:
                roots[cx] = made
        if nodes > 1:
            saved, base = leaf_pairs, n_cy - 2 * nodes
    for j in range(1, n_cx):
        root_copy(j).start()

    forward(0)
    def sibling_at(level):
        mine = lax.div(cy, 1 << (level - 1))
        return mine + 1 - 2 * lax.rem(mine, 2)

    base = 0
    nodes = n_cy
    for level in range(1, up_group + 1):
        if level == 1:
            sibling = group[sibling_at(level)]
        else:
            sibling = leaf_pairs[base + sibling_at(level)]
        terms.append(path_term(level, sibling))
        nodes //= 2
        base = n_cy - 2 * nodes

    get_near.wait()

    def near_dot(tile, block):
        return lax.dot_general(
            tile, block, (((1,), (1,)), ((), ())), preferred_element_type=F32
        )

    def own_near(g, _):
        acc[g] = near_dot(win_cols[REACH * leaves + g], near_v[g, 0])
        return 0

    lax.fori_loop(0, leaves, own_near, 0)

    for u in range(1, CHUNKS - 1):
        forward(u)
    finish(CHUNKS)
    mate_copy(win_skel, 1).wait_recv()
    last(CHUNKS)
    get_far.wait()
    first = (me - REACH) * leaves

    def slot_of(leaf_id):
        return jnp.clip(leaf_id - first, 0, (2 * REACH + 1) * leaves - 1)

    high_row = (lax.broadcasted_iota(jnp.int32, (1, 2 * cols), 1) >= cols).astype(F32)
    for g in range(leaves):
        total = None
        for k in range(kfar):
            index = slot_of(far_ids[g, k])
            parity = (index & 1).astype(F32)
            keep = (parity * high_row + (1.0 - parity) * (1.0 - high_row)).astype(BF16)
            term = dot(far_v[g, k], win_skel[index >> 1] * keep)
            total = term if total is None else total + term
        far_sum[g] = total

    forward(CHUNKS - 1)
    for u in range(CHUNKS - 2):
        finish(u)

    for j in range(1, n_cx):
        root_arrival(j).wait_recv()

    if n_cx > 1:
        for x in range(n_cx):
            leaf_pairs[n_cy + x] = roots[x]
        base, nodes = n_cy, n_cx
        fresh = n_cy + n_cx
        for level in range(up_group + 1, up_all + 1):
            mine = lax.div(cx, 1 << (level - up_group - 1))
            sibling = leaf_pairs[base + mine + 1 - 2 * lax.rem(mine, 2)]
            terms.append(path_term(level, sibling))
            nodes //= 2
            if nodes > 1:
                for m in range(nodes):
                    leaf_pairs[fresh + m] = up(
                        upper_v[starts[level - 1] + m],
                        leaf_pairs[base + 2 * m],
                        leaf_pairs[base + 2 * m + 1],
                    )
                base = fresh
                fresh += nodes

    coef = terms[-1]
    for level in range(up_all - 1, 0, -1):
        right = lax.rem(lax.div(me, 1 << (level - 1)), 2)
        rows = path_down[level - 1, pl.ds(pl.multiple_of(right * rank, rank), rank)]
        coef = fold(dot(rows, pack(coef))) + terms[level - 1]
    coefs = [coef]
    width = 1
    row = leaves - 1
    while width < leaves:
        row -= width
        following = []
        for m in range(width):
            made = fold2(dot(local_down[row + m], pack(coefs[m])), cols)
            following += [made[:rank], made[rank:]]
        coefs = following
        width *= 2

    for g in range(leaves):
        coef_half = (coefs[g] + fold(far_sum[g]))[:, :cols].astype(BF16)
        acc[g] = acc[g] + dot_t(coef_half, basis_v[g])

    for u in range(CHUNKS - 2, CHUNKS):
        finish(u)
    mate_copy(win_cols, 0).wait_recv()
    for u in range(CHUNKS):
        last(u)

    def far_near(g, _):
        total = acc[g]
        for k in range(1, knear):
            total = total + near_dot(win_cols[slot_of(near_ids[k, g])], near_v[g, k])
        out[g] = total.astype(BF16)
        return 0

    lax.fori_loop(0, leaves, far_near, 0)

    for u in range(CHUNKS + 1):
        x_copy(u).wait_send()

        @pl.when(onward)
        def _(u=u):
            y_copy(u).wait_send()

        @pl.when(relays)
        def _(u=u):
            relay_copy(u).wait_send()

    mate_copy(win_skel, 1).wait_send()
    mate_copy(win_cols, 0).wait_send()
    for j in range(1, n_cy):
        group_copy(j).wait_send()
    for j in range(1, n_cx):
        root_copy(j).wait_send()


def fold2(x, cols):
    return x + pltpu.roll(x, cols, 1)


def solution(mesh):
    n_cx, n_cy = mesh.shape["cx"], mesh.shape["cy"]
    n = n_cx * n_cy

    def local(
        points, basis, near, near_ids, local_transfer, far, far_ids, upper_transfer, upper_coupling
    ):
        leaves, cols, leaf = points.shape
        rank = basis.shape[1]
        local_turned = jnp.swapaxes(local_transfer, 1, 2)
        upper_turned = jnp.swapaxes(upper_transfer, 1, 2)
        up_group, up_all = levels_of(n_cy), levels_of(n)
        window = 2 * REACH + 1
        kept = n_cy + n_cx
        any_space = pl.BlockSpec(memory_space=pl.ANY)
        dma = pltpu.SemaphoreType.DMA
        return pl.pallas_call(
            functools.partial(kernel, n_cx, n_cy),
            out_shape=jax.ShapeDtypeStruct(points.shape, points.dtype),
            in_specs=[pl.BlockSpec(memory_space=pltpu.SMEM)] * 2 + [any_space] * 7,
            out_specs=pl.BlockSpec(memory_space=pltpu.VMEM),
            scratch_shapes=[
                pltpu.VMEM((window * leaves, cols, leaf), BF16),
                pltpu.VMEM((window * leaves // 2, rank, 2 * cols), BF16),
                pltpu.VMEM(basis.shape, BF16),
                pltpu.VMEM(near.shape, BF16),
                pltpu.VMEM(local_turned.shape, BF16),
                pltpu.VMEM(far.shape, BF16),
                pltpu.VMEM((kept,) + upper_turned.shape[1:], BF16),
                pltpu.VMEM((up_all,) + upper_coupling.shape[1:], BF16),
                pltpu.VMEM((leaves, cols, leaf), F32),
                pltpu.VMEM(local_transfer.shape, BF16),
                pltpu.VMEM((up_all,) + upper_transfer.shape[1:], BF16),
                pltpu.VMEM((leaves, rank, 2 * cols), F32),
                pltpu.VMEM((n_cy + 2 * n_cx, rank, 2 * cols), BF16),
                pltpu.VMEM((n_cy, rank, 2 * cols), BF16),
                pltpu.VMEM((n_cx, rank, 2 * cols), BF16),
                dma((5 + 2 * up_all,)),
                dma((CHUNKS + 1,)),
                dma((CHUNKS + 1,)),
                dma((CHUNKS + 1,)),
                dma((CHUNKS + 1,)),
                dma((2,)),
                dma((2,)),
                dma((CHUNKS + 1,)),
                dma((CHUNKS + 1,)),
                dma((n_cy,)),
                dma((n_cy,)),
                dma((n_cx,)),
                dma((n_cx,)),
            ],
            compiler_params=pltpu.CompilerParams(
                collective_id=0, has_side_effects=True, vmem_limit_bytes=56 * 2**20
            ),
        )(near_ids.T, far_ids, points, basis, near, local_turned, far, upper_turned, upper_coupling)

    split = ("cx", "cy")
    return jax.shard_map(
        local,
        mesh=mesh,
        in_specs=(
            P(split, None, None),
            P(split, None, None),
            P(split, None, None, None),
            P(split, None),
            P(split, None, None),
            P(split, None, None, None),
            P(split, None),
            P(),
            P(),
        ),
        out_specs=P(split, None, None),
        check_vma=False,
    )
```
